512 devices in a mesh: lon: 64 (over x, y_lo, z), lev: 8 (over y_hi, core).
Axes of the slice: x: 4, y: 8 (y_hi: 4, y_lo: 2; y = y_hi * 2 + y_lo), z: 8, core: 2. Of those that a mesh axis runs over, the one named last changes fastest.
Arguments:
- cotangent: float32 [5, 8, 2880, 1024], P(None, 'lev', 'lon'), may hold values from -6 to 6
- zonal_coef: float32 [8, 2880, 1024], P('lev', 'lon'), may hold values from -0.5 to 0.5
- merid_coef: float32 [8, 2880, 1024], P('lev', 'lon'), may hold values from -0.5 to 0.5
- vertical_wind: float32 [8, 2880, 1024], P('lev', 'lon'), may hold values from -0.5 to 0.5
- cutoff: int32 [64], replicated, may hold values from 1 to 360, as said below
Outputs:
- adjoint_state: float32 [5, 8, 2880, 1024], P(None, 'lev', 'lon')
The draws below stay inside these ranges and needn't reach their ends.
Inputs may be any that keep to these rules, and one draw needn't show every extreme that they name: Every draw holds a row with cutoff exactly 360 and a row with cutoff exactly 1.
All inputs are finite; a program needn't handle non-finite values.
Results may differ from the reference program's by a relative error of at most 0.00023.
Values sent between devices are 32-bit elements; how exact they have to be, the bound alone decides.
No kernel may reach another device: no remote copies, remote signals or barrier semaphores. Data moves between devices by JAX's collectives and lax.ppermute only.
A program may use at most 64 MiB of HBM per device.

```python
import jax
import jax.numpy as jnp

NLON = 2880
NLEV = 8
NLAT = 1024
POLAR = 32
KMAX = 360


def draw_cutoff(key, part):
    first_key, second_key, third_key = jax.random.split(jax.random.fold_in(key, 17), 3)
    values = jax.random.randint(first_key, (2 * POLAR,), 1, KMAX + 1)
    position = jax.random.randint(second_key, (), 0, 2 * POLAR)
    offset = jax.random.randint(third_key, (), 1, 2 * POLAR)
    values = values.at[position].set(KMAX)
    values = values.at[(position + offset) % (2 * POLAR)].set(1)
    return values.astype(jnp.int32)


def level_of(stream_key, shape, shards, smallest, high):
    level = 1.0
    for axis_at, parts in shards:
        heights = jax.random.uniform(jax.random.fold_in(jax.random.fold_in(stream_key, 6), axis_at), (parts,), jnp.float32, smallest / len(shards), high / len(shards))
        level = level * jnp.repeat(jnp.exp(heights), shape[axis_at] // parts).reshape((-1,) + (1,) * (len(shape) - 1 - axis_at))
    return level


def normal_values(rng, extent, width, bound, cuts=(), kind=jnp.bfloat16):
    loudness = level_of(rng, extent, cuts, -0.22, 0.18) if cuts else 1.0
    entries = jax.random.normal(rng, extent, jnp.float32) * width * loudness
    return jnp.minimum(jnp.maximum(entries, -bound), bound).astype(kind)


def setup_inputs(seed: int = 0) -> dict:
    key_of = jax.random.split(jax.random.key(seed), 6)
    return {
        "cotangent": normal_values(key_of[0], (5, NLEV, NLON, NLAT), 1.0, 6.0, ((1, 8), (2, 64)), jnp.float32),
        "zonal_coef": jnp.clip(jax.random.uniform(key_of[1], (NLEV, NLON, NLAT), jnp.float32, -0.5, 0.5) * level_of(key_of[1], (NLEV, NLON, NLAT), ((0, 8), (1, 64)), -0.4, 0.0), -0.5, 0.5),
        "merid_coef": jnp.clip(jax.random.uniform(key_of[2], (NLEV, NLON, NLAT), jnp.float32, -0.5, 0.5) * level_of(key_of[2], (NLEV, NLON, NLAT), ((0, 8), (1, 64)), -0.4, 0.0), -0.5, 0.5),
        "vertical_wind": jnp.clip(jax.random.uniform(key_of[3], (NLEV, NLON, NLAT), jnp.float32, -0.5, 0.5) * level_of(key_of[3], (NLEV, NLON, NLAT), ((0, 8), (1, 64)), -0.4, 0.0), -0.5, 0.5),
        "cutoff": draw_cutoff(jax.random.fold_in(key_of[5], 71), 0),
    }


COUPLE_G = 0.3
COUPLE_H = 0.3
COUPLE_B = 0.2


def diff_lon(field):
    return jnp.roll(field, -1, axis=2) - jnp.roll(field, 1, axis=2)


def diff_lat(field):
    padded = jnp.pad(field, ((0, 0), (0, 0), (0, 0), (1, 1)))
    return padded[..., 2:] - padded[..., :-2]


def reference(cotangent, zonal_coef, merid_coef, vertical_wind, cutoff):
    weighted = vertical_wind[None] * cotangent
    padded = jnp.pad(weighted, ((0, 0), (1, 1), (0, 0), (0, 0)))
    adjoint_one = cotangent + (padded[:, 2:] - padded[:, :-2])
    below_sums = jnp.flip(jnp.cumsum(jnp.flip(cotangent[2], 0), 0), 0)
    adjoint_one = adjoint_one.at[3].add(-COUPLE_B * below_sums)
    polar_rows = jnp.concatenate([adjoint_one[..., :POLAR], adjoint_one[..., NLAT - POLAR:]], axis=3)
    spectrum = jnp.fft.rfft(polar_rows, axis=2)
    wavenum = jnp.arange(NLON // 2 + 1, dtype=jnp.int32)[:, None]
    keep_mask = wavenum <= cutoff[None, :]
    spectrum = jnp.where(keep_mask[None, None], spectrum, 0.0)
    smoothed = jnp.fft.irfft(spectrum, n=NLON, axis=2).astype(adjoint_one.dtype)
    filtered = jnp.concatenate([smoothed[..., :POLAR], adjoint_one[..., POLAR:NLAT - POLAR], smoothed[..., POLAR:]], axis=3)
    zonal_part = zonal_coef[None] * filtered
    zonal_flux = jnp.stack([zonal_part[0] + COUPLE_H * filtered[3], zonal_part[1], zonal_part[2], zonal_part[3] + COUPLE_G * filtered[0], zonal_part[4]])
    merid_part = merid_coef[None] * filtered
    merid_flux = jnp.stack([merid_part[0], merid_part[1] + COUPLE_H * filtered[3], merid_part[2], merid_part[3] + COUPLE_G * filtered[1], merid_part[4]])
    return adjoint_one + diff_lon(zonal_flux) + diff_lat(merid_flux)
```

```python
import math

import jax
import jax.numpy as jnp
import numpy as np
from jax import lax
from jax.experimental import pallas as pl
from jax.experimental.pallas import tpu as pltpu
from jax.sharding import PartitionSpec as P

NLON = 2880
LON = 45
DEVS = NLON // LON
LEVS = 8
NLAT = 1024
POLAR = 32
FIELDS = 5
LANES = 128
TILES = NLAT // LANES
SHARE = (LON + 1) // 2
HALF = 24
ROWS = 2 * HALF
PACK = HALF + 2 * TILES
FULL = TILES * LON
WAVES = 6

COUPLE_G = 0.3
COUPLE_H = 0.3
COUPLE_B = 0.2

HIGHEST = lax.Precision.HIGHEST


def lane_index(shape):
    return lax.broadcasted_iota(jnp.int32, shape, len(shape) - 1)


def row_index(shape):
    return lax.broadcasted_iota(jnp.int32, shape, len(shape) - 2)


def polar_mask(shape):
    lane, tile = lane_index(shape), row_index(shape) % TILES
    return ((tile == 0) & (lane < POLAR)) | ((tile == TILES - 1) & (lane >= LANES - POLAR))


def pack_polar(first, last):
    lane = lane_index((LON, LANES))
    both = jnp.where(lane < LANES // 2, first, last)
    both = jnp.concatenate([both, jnp.zeros((ROWS - LON, LANES), both.dtype)], axis=0)
    lane = lane[:HALF]
    outer = (lane < POLAR) | (lane >= LANES - POLAR)
    return jnp.where(outer, both[:HALF], pltpu.roll(both[HALF:], LANES // 2, 1))


def pack_kernel(c_ref, w_ref, inner_ref, outer_ref, rest_ref, own_ref, theta_ref, below_ref):
    rows = [slice(f * PACK, f * PACK + HALF) for f in range(FIELDS)]
    lows = [slice(f * PACK + HALF, f * PACK + HALF + TILES) for f in range(FIELDS)]
    highs = [slice(f * PACK + HALF + TILES, (f + 1) * PACK) for f in range(FIELDS)]
    w = w_ref[...]
    w_first, w_last = w_ref[:, 0, :], w_ref[:, TILES - 1, :]
    for f in range(FIELDS):
        field = c_ref[f]
        first, last = c_ref[f, :, 0, :], c_ref[f, :, TILES - 1, :]
        own_ref[rows[f], :] = pack_polar(first, last)
        own_ref[lows[f], :] = field[0]
        own_ref[highs[f], :] = field[LON - 1]
        if f == 2:
            packed = own_ref[f * PACK : (f + 1) * PACK, :]
            for k in range(LEVS):
                theta_ref[k] = packed
            inner_ref[FIELDS * (PACK + FULL) :, :] = field.reshape(FULL, LANES)
            below_ref[...] = field
        weighted = w * field
        whole = weighted.reshape(FULL, LANES)
        polar = pack_polar(w_first * first, w_last * last)
        at = FIELDS * PACK + f * FULL
        inner_ref[at : at + FULL, :] = whole
        for ref in (inner_ref, outer_ref):
            ref[rows[f], :] = polar
            ref[lows[f], :] = weighted[0]
            ref[highs[f], :] = weighted[LON - 1]
        rest_ref[f * FULL : (f + 1) * FULL, :] = whole


def level_signs():
    level = lax.axis_index("lev")
    even = level % 2 == 0
    inner = jnp.where(even, 1.0, -1.0).astype(jnp.float32)
    outer = jnp.where((level == 0) | (level == LEVS - 1), 0.0, -inner).astype(jnp.float32)
    return level, inner, outer


def below_sum(level, value_of):
    total = jnp.where(level <= 0, value_of(0), 0.0)
    for m in range(1, LEVS):
        total = total + jnp.where(m >= level, value_of(m), 0.0)
    return total


def zonal_fluxes(coef, field):
    flux = [coef * x for x in field]
    flux[0] = flux[0] + COUPLE_H * field[3]
    flux[3] = flux[3] + COUPLE_G * field[0]
    return flux


def pair_half(core):
    return pl.ds((LON - SHARE) * core, SHARE)


def pair_kernel(below_ref, inner_ref, pair_ref):
    core = lax.axis_index("lev") % 2
    other = inner_ref[FIELDS * (PACK + FULL) :, :].reshape(LON, TILES, LANES)
    both = below_ref[...] + other
    pair_ref[...] = jnp.where(core == 0, both[:SHARE], both[LON - SHARE :])


def merge_kernel(own_ref, zc_ref, inner_ref, outer_ref, theta_ref, out_ref):
    level, inner, outer = level_signs()
    adjoint = []
    for f in range(FIELDS):
        at = slice(f * PACK, (f + 1) * PACK)
        adjoint.append(own_ref[at, :] + inner * inner_ref[at, :] + outer * outer_ref[at, :])
    adjoint[3] = adjoint[3] - COUPLE_B * below_sum(level, lambda m: theta_ref[m])
    rows = [a[:HALF] for a in adjoint]
    rows.append(jnp.zeros((LANES - FIELDS * HALF, LANES), jnp.float32))
    turned = jnp.concatenate(rows, axis=0).T
    out_ref[:POLAR, 0, :] = turned[:POLAR]
    out_ref[POLAR:, 0, :] = turned[LANES - POLAR :]
    out_ref[:POLAR, 1, :] = turned[2 * POLAR : 3 * POLAR]
    out_ref[POLAR:, 1, :] = turned[POLAR : 2 * POLAR]
    coef = jnp.concatenate([zc_ref[0], zc_ref[LON - 1]], axis=0)
    flux = zonal_fluxes(coef, [a[HALF:] for a in adjoint])
    flux[0] = jnp.where(polar_mask(coef.shape), coef, flux[0])
    edges = jnp.concatenate([x[TILES:] for x in flux] + [x[:TILES] for x in flux], axis=0)
    out_ref[:, 2, :] = edges[:DEVS]
    left = 2 * FIELDS * TILES - DEVS
    out_ref[:left, 3, :] = edges[DEVS:]
    out_ref[left:, 3, :] = jnp.zeros((DEVS - left, LANES), jnp.float32)


def filter_tables():
    dev = np.arange(DEVS)
    lane = np.arange(2 * LANES)
    place = (lane % LANES) % HALF + HALF * (lane // LANES)
    used = (lane % LANES) < FIELDS * HALF
    field = np.where(used, (lane % LANES) // HALF, -1)
    wave_field = np.arange(LANES // 2) // WAVES
    wave = np.arange(LANES // 2) % WAVES
    circle = 2 * math.pi * np.outer(dev, dev) / DEVS

    def twiddle(offset):
        angle = 2 * math.pi * np.outer(dev, place + offset) / NLON
        return np.concatenate([np.cos(angle), np.sin(angle)], axis=0)

    def short(offset, keep):
        angle = 2 * math.pi * np.outer(place + offset, wave) / LON
        same = (field[:, None] == wave_field[None, :]) & keep[:, None]
        return np.cos(angle) * same, np.sin(angle) * same

    inside = used & (place < LON)
    cos_in, sin_in = short(0, inside)
    cos_out, sin_out = short(-1, used)
    forward_dev = np.concatenate([np.cos(circle), np.sin(circle)], axis=0)
    forward_lon = np.concatenate(
        [np.concatenate([cos_in, -sin_in], 1), np.concatenate([sin_in, cos_in], 1)], axis=0
    )
    back_lon = np.concatenate(
        [np.concatenate([cos_out.T, sin_out.T], 1), np.concatenate([-sin_out.T, cos_out.T], 1)], axis=0
    )
    back_dev = np.concatenate([np.cos(circle), -np.sin(circle)], axis=1)
    tables = (forward_dev, np.concatenate([twiddle(0), twiddle(-1)], 0), forward_lon, back_lon, back_dev)
    return [np.asarray(t, np.float32) for t in tables]


def dot(a, b):
    return jnp.dot(a, b, precision=HIGHEST, preferred_element_type=jnp.float32)


def filter_kernel(cut_ref, in_ref, dev_ref, twiddle_ref, lon_ref, back_lon_ref, back_dev_ref, out_ref):
    me = lax.axis_index("lon")
    cut = cut_ref[me]
    values = jnp.concatenate([in_ref[:, 0, :], in_ref[:, 1, :]], axis=1)
    split = dot(dev_ref[...], values)
    real, sine = split[:DEVS], split[DEVS:]
    cos, sin = twiddle_ref[:DEVS, :], twiddle_ref[DEVS : 2 * DEVS, :]
    turned = jnp.concatenate([real * cos - sine * sin, -(real * sin + sine * cos)], axis=1)
    waves = dot(turned, lon_ref[...])
    lane = lane_index(waves.shape)
    number = row_index(waves.shape) + DEVS * ((lane % (LANES // 2)) % WAVES)
    weight = jnp.where(number == 0, 1.0 / NLON, 2.0 / NLON)
    waves = jnp.where(number <= cut, waves * weight, 0.0)
    back = dot(waves, back_lon_ref[...])
    real, imag = back[:, : 2 * LANES], back[:, 2 * LANES :]
    cos, sin = twiddle_ref[2 * DEVS : 3 * DEVS, :], twiddle_ref[3 * DEVS :, :]
    turned = jnp.concatenate([real * cos - imag * sin, real * sin + imag * cos], axis=0)
    smooth = dot(back_dev_ref[...], turned)
    out_ref[:, 0, :] = smooth[:, :LANES]
    out_ref[:, 1, :] = smooth[:, LANES:]
    edge = in_ref[:, 2, :]
    right = pltpu.roll(edge, 1, 0)
    left = pltpu.roll(edge, DEVS - 1, 0)
    out_ref[:, 2, :] = jnp.where(me < FIELDS * TILES, right, left)
    out_ref[:, 3, :] = pltpu.roll(in_ref[:, 3, :], DEVS - 1, 0)


def final_kernel(c_ref, zc_ref, mc_ref, inner_ref, rest_ref, mine_ref, theirs_ref, back_ref, out_ref, adj_ref, fil_ref):
    level, inner, outer = level_signs()
    core = level % 2
    partner = jnp.where(core == 0, 1.0, 0.0).astype(jnp.float32)
    adj_ref[3, pair_half(core)] = mine_ref[...]
    adj_ref[3, pair_half(1 - core)] = theirs_ref[...]
    shape = (LON, TILES, LANES)

    def part(ref, at):
        return ref[at : at + FULL, :].reshape(shape)

    turned = jnp.concatenate(
        [back_ref[:POLAR, 0, :], back_ref[POLAR:, 1, :], back_ref[:POLAR, 1, :], back_ref[POLAR:, 0, :]], axis=0
    ).T
    lane = lane_index((LON, LANES))
    halos = []
    for f in range(FIELDS):
        value = c_ref[f] + inner * part(inner_ref, FIELDS * PACK + f * FULL) + outer * part(rest_ref, f * FULL)
        if f == 3:
            below = c_ref[2] + partner * part(inner_ref, FIELDS * (PACK + FULL)) + adj_ref[3]
            value = value - COUPLE_B * below
        adj_ref[f] = value
        fil_ref[f] = value
        ring = turned[f * HALF : (f + 1) * HALF]
        ring = jnp.concatenate([ring, pltpu.roll(ring, LANES // 2, 1)], axis=0)
        halos.append((ring[0:1], ring[LON + 1 : LON + 2]))
        ring = pltpu.roll(ring, ROWS - 1, 0)[:LON]
        fil_ref[f, :, 0, :] = jnp.where(lane < POLAR, ring, adj_ref[f, :, 0, :])
        fil_ref[f, :, TILES - 1, :] = jnp.where(lane >= LANES - POLAR, ring, adj_ref[f, :, TILES - 1, :])

    polar = polar_mask((TILES, LANES))

    def edge_fluxes(side):
        tiles = []
        for f in range(FIELDS):
            q = (side * FIELDS + f) * TILES
            tiles.append(back_ref[q : q + TILES, 2, :] if q < DEVS else back_ref[q - DEVS : q - DEVS + TILES, 3, :])
        ring = zonal_fluxes(tiles[0], [h[side] for h in halos])
        return [jnp.where(polar, a, b)[None] for a, b in zip(ring, tiles)]

    west, east = edge_fluxes(0), edge_fluxes(1)
    lane, tile = lane_index(shape), row_index(shape)
    for f in range(FIELDS):
        field = fil_ref[f]
        zonal = zc_ref[...] * field
        merid = mc_ref[...] * field
        if f == 0:
            zonal = zonal + COUPLE_H * fil_ref[3]
        if f == 1:
            merid = merid + COUPLE_H * fil_ref[3]
        if f == 3:
            zonal = zonal + COUPLE_G * fil_ref[0]
            merid = merid + COUPLE_G * fil_ref[1]
        after = jnp.concatenate([zonal[1:], east[f]], axis=0)
        before = jnp.concatenate([west[f], zonal[:-1]], axis=0)
        north = pltpu.roll(merid, LANES - 1, 2)
        carry = jnp.where(tile == TILES - 1, 0.0, pltpu.roll(north, TILES - 1, 1))
        north = jnp.where(lane == LANES - 1, carry, north)
        south = pltpu.roll(merid, 1, 2)
        carry = jnp.where(tile == 0, 0.0, pltpu.roll(south, 1, 1))
        south = jnp.where(lane == 0, carry, south)
        out_ref[f] = adj_ref[f] + (after - before) + (north - south)


def call(kernel, out_shape, *args, spaces={}, scratch=(), vmem_mib=8):
    specs = [pl.BlockSpec(memory_space=spaces.get(i, pltpu.VMEM)) for i in range(len(args))]
    return pl.pallas_call(
        kernel,
        out_shape=out_shape,
        in_specs=specs,
        out_specs=jax.tree.map(lambda _: pl.BlockSpec(memory_space=pltpu.VMEM), out_shape),
        scratch_shapes=scratch,
        compiler_params=pltpu.CompilerParams(vmem_limit_bytes=vmem_mib * 2**20),
        cost_estimate=pl.CostEstimate(flops=2**20, bytes_accessed=6 * 2**20, transcendentals=0),
    )(*args)


def array(*shape):
    return jax.ShapeDtypeStruct(shape, jnp.float32)


def body(cotangent, zonal_coef, merid_coef, vertical_wind, cutoff):
    cotangent = cotangent.reshape(FIELDS, LON, TILES, LANES)
    zonal_coef, merid_coef, vertical_wind = (
        a.reshape(LON, TILES, LANES) for a in (zonal_coef, merid_coef, vertical_wind)
    )
    inner, outer, rest, own, theta, below = call(
        pack_kernel,
        (
            array(FIELDS * (PACK + FULL) + FULL, LANES),
            array(FIELDS * PACK, LANES),
            array(FIELDS * FULL, LANES),
            array(FIELDS * PACK, LANES),
            array(LEVS, PACK, LANES),
            array(LON, TILES, LANES),
        ),
        cotangent,
        vertical_wind,
    )
    pairs = [(k, k ^ 1) for k in range(LEVS)]
    crossing = [(k, ((k + 1) ^ 1) - 1) for k in range(1, LEVS - 1)]
    inner = lax.ppermute(inner, "lev", pairs)
    outer = lax.ppermute(outer, "lev", crossing)

    def hand_down(values, levels):
        return lax.ppermute(values, "lev", [(k, k - levels) for k in range(levels, LEVS)])

    theta = lax.all_to_all(theta, "lev", 0, 0, tiled=True)
    pair = call(pair_kernel, array(SHARE, TILES, LANES), below, inner)
    one = hand_down(pair, 2)
    sent = call(merge_kernel, array(DEVS, 4, LANES), own, zonal_coef, inner, outer, theta)
    sent, one = lax.optimization_barrier((sent, one))
    two = hand_down(pair + one, 4)
    circle = lax.all_to_all(sent, "lon", 0, 0, tiled=True)
    circle, rest = lax.optimization_barrier((circle, rest))
    rest = lax.ppermute(rest, "lev", crossing)
    smooth = call(
        filter_kernel, array(DEVS, 4, LANES), cutoff, circle, *filter_tables(), spaces={0: pltpu.SMEM}
    )
    back = lax.all_to_all(smooth, "lon", 0, 0, tiled=True)
    mine = one + two
    theirs = lax.ppermute(mine, "lev", pairs)
    out = call(
        final_kernel,
        array(FIELDS, LON, TILES, LANES),
        cotangent,
        zonal_coef,
        merid_coef,
        inner,
        rest,
        mine,
        theirs,
        back,
        scratch=[pltpu.VMEM((FIELDS, LON, TILES, LANES), jnp.float32)] * 2,
        vmem_mib=24,
    )
    return out.reshape(FIELDS, 1, LON, NLAT)


def solution(mesh):
    return jax.shard_map(
        body,
        mesh=mesh,
        in_specs=(
            P(None, "lev", "lon", None),
            P("lev", "lon", None),
            P("lev", "lon", None),
            P("lev", "lon", None),
            P(),
        ),
        out_specs=P(None, "lev", "lon", None),
        check_vma=False,
    )
```

```python
import math

import jax
import jax.numpy as jnp
import numpy as np
from jax import lax
from jax.experimental import pallas as pl
from jax.experimental.pallas import tpu as pltpu
from jax.sharding import PartitionSpec as P

NLON = 2880
LON = 45
DEVS = NLON // LON
LEVS = 8
NLAT = 1024
POLAR = 32
FIELDS = 5
LANES = 128
TILES = NLAT // LANES
SHARE = (LON + 1) // 2
HALF = 24
ROWS = 2 * HALF
PACK = HALF + 2 * TILES
FULL = TILES * LON
WAVES = 6

COUPLE_G = 0.3
COUPLE_H = 0.3
COUPLE_B = 0.2

HIGHEST = lax.Precision.HIGHEST


def lane_index(shape):
    return lax.broadcasted_iota(jnp.int32, shape, len(shape) - 1)


def row_index(shape):
    return lax.broadcasted_iota(jnp.int32, shape, len(shape) - 2)


def polar_mask(shape):
    lane, tile = lane_index(shape), row_index(shape) % TILES
    return ((tile == 0) & (lane < POLAR)) | ((tile == TILES - 1) & (lane >= LANES - POLAR))


def pack_polar(first, last):
    lane = lane_index((LON, LANES))
    both = jnp.where(lane < LANES // 2, first, last)
    both = jnp.concatenate([both, jnp.zeros((ROWS - LON, LANES), both.dtype)], axis=0)
    lane = lane[:HALF]
    outer = (lane < POLAR) | (lane >= LANES - POLAR)
    return jnp.where(outer, both[:HALF], pltpu.roll(both[HALF:], LANES // 2, 1))


def pack_kernel(c_ref, w_ref, inner_ref, outer_ref, rest_ref, own_ref, theta_ref, below_ref):
    rows = [slice(f * PACK, f * PACK + HALF) for f in range(FIELDS)]
    lows = [slice(f * PACK + HALF, f * PACK + HALF + TILES) for f in range(FIELDS)]
    highs = [slice(f * PACK + HALF + TILES, (f + 1) * PACK) for f in range(FIELDS)]
    w = w_ref[...]
    w_first, w_last = w_ref[:, 0, :], w_ref[:, TILES - 1, :]
    for f in range(FIELDS):
        field = c_ref[f]
        first, last = c_ref[f, :, 0, :], c_ref[f, :, TILES - 1, :]
        own_ref[rows[f], :] = pack_polar(first, last)
        own_ref[lows[f], :] = field[0]
        own_ref[highs[f], :] = field[LON - 1]
        if f == 2:
            packed = own_ref[f * PACK : (f + 1) * PACK, :]
            for k in range(LEVS):
                theta_ref[k] = packed
            inner_ref[FIELDS * (PACK + FULL) :, :] = field.reshape(FULL, LANES)
            below_ref[...] = field
        weighted = w * field
        whole = weighted.reshape(FULL, LANES)
        polar = pack_polar(w_first * first, w_last * last)
        at = FIELDS * PACK + f * FULL
        inner_ref[at : at + FULL, :] = whole
        for ref in (inner_ref, outer_ref):
            ref[rows[f], :] = polar
            ref[lows[f], :] = weighted[0]
            ref[highs[f], :] = weighted[LON - 1]
        rest_ref[f * FULL : (f + 1) * FULL, :] = whole


def level_signs():
    level = lax.axis_index("lev")
    even = level % 2 == 0
    inner = jnp.where(even, 1.0, -1.0).astype(jnp.float32)
    outer = jnp.where((level == 0) | (level == LEVS - 1), 0.0, -inner).astype(jnp.float32)
    return level, inner, outer


def below_sum(level, value_of):
    total = jnp.where(level <= 0, value_of(0), 0.0)
    for m in range(1, LEVS):
        total = total + jnp.where(m >= level, value_of(m), 0.0)
    return total


def zonal_fluxes(coef, field):
    flux = [coef * x for x in field]
    flux[0] = flux[0] + COUPLE_H * field[3]
    flux[3] = flux[3] + COUPLE_G * field[0]
    return flux


def pair_half(core):
    return pl.ds((LON - SHARE) * core, SHARE)


def pair_kernel(below_ref, inner_ref, pair_ref):
    core = lax.axis_index("lev") % 2
    other = inner_ref[FIELDS * (PACK + FULL) :, :].reshape(LON, TILES, LANES)
    both = below_ref[...] + other
    pair_ref[...] = jnp.where(core == 0, both[:SHARE], both[LON - SHARE :])


def merge_kernel(own_ref, zc_ref, inner_ref, outer_ref, theta_ref, out_ref):
    level, inner, outer = level_signs()
    adjoint = []
    for f in range(FIELDS):
        at = slice(f * PACK, (f + 1) * PACK)
        adjoint.append(own_ref[at, :] + inner * inner_ref[at, :] + outer * outer_ref[at, :])
    adjoint[3] = adjoint[3] - COUPLE_B * below_sum(level, lambda m: theta_ref[m])
    rows = [a[:HALF] for a in adjoint]
    rows.append(jnp.zeros((LANES - FIELDS * HALF, LANES), jnp.float32))
    turned = jnp.concatenate(rows, axis=0).T
    out_ref[:POLAR, 0, :] = turned[:POLAR]
    out_ref[POLAR:, 0, :] = turned[LANES - POLAR :]
    out_ref[:POLAR, 1, :] = turned[2 * POLAR : 3 * POLAR]
    out_ref[POLAR:, 1, :] = turned[POLAR : 2 * POLAR]
    coef = jnp.concatenate([zc_ref[0], zc_ref[LON - 1]], axis=0)
    flux = zonal_fluxes(coef, [a[HALF:] for a in adjoint])
    flux[0] = jnp.where(polar_mask(coef.shape), coef, flux[0])
    edges = jnp.concatenate([x[TILES:] for x in flux] + [x[:TILES] for x in flux], axis=0)
    out_ref[:, 2, :] = edges[:DEVS]
    left = 2 * FIELDS * TILES - DEVS
    out_ref[:left, 3, :] = edges[DEVS:]
    out_ref[left:, 3, :] = jnp.zeros((DEVS - left, LANES), jnp.float32)


def filter_tables():
    dev = np.arange(DEVS)
    lane = np.arange(2 * LANES)
    place = (lane % LANES) % HALF + HALF * (lane // LANES)
    used = (lane % LANES) < FIELDS * HALF
    field = np.where(used, (lane % LANES) // HALF, -1)
    wave_field = np.arange(LANES // 2) // WAVES
    wave = np.arange(LANES // 2) % WAVES
    circle = 2 * math.pi * np.outer(dev, dev) / DEVS

    def twiddle(offset):
        angle = 2 * math.pi * np.outer(dev, place + offset) / NLON
        return np.concatenate([np.cos(angle), np.sin(angle)], axis=0)

    def short(offset, keep):
        angle = 2 * math.pi * np.outer(place + offset, wave) / LON
        same = (field[:, None] == wave_field[None, :]) & keep[:, None]
        return np.cos(angle) * same, np.sin(angle) * same

    inside = used & (place < LON)
    cos_in, sin_in = short(0, inside)
    cos_out, sin_out = short(-1, used)
    forward_dev = np.concatenate([np.cos(circle), np.sin(circle)], axis=0)
    forward_lon = np.concatenate(
        [np.concatenate([cos_in, -sin_in], 1), np.concatenate([sin_in, cos_in], 1)], axis=0
    )
    back_lon = np.concatenate(
        [np.concatenate([cos_out.T, sin_out.T], 1), np.concatenate([-sin_out.T, cos_out.T], 1)], axis=0
    )
    back_dev = np.concatenate([np.cos(circle), -np.sin(circle)], axis=1)
    tables = (forward_dev, np.concatenate([twiddle(0), twiddle(-1)], 0), forward_lon, back_lon, back_dev)
    return [np.asarray(t, np.float32) for t in tables]


def dot(a, b):
    return jnp.dot(a, b, precision=HIGHEST, preferred_element_type=jnp.float32)


def filter_kernel(cut_ref, in_ref, dev_ref, twiddle_ref, lon_ref, back_lon_ref, back_dev_ref, out_ref):
    me = lax.axis_index("lon")
    cut = cut_ref[me]
    values = jnp.concatenate([in_ref[:, 0, :], in_ref[:, 1, :]], axis=1)
    split = dot(dev_ref[...], values)
    real, sine = split[:DEVS], split[DEVS:]
    cos, sin = twiddle_ref[:DEVS, :], twiddle_ref[DEVS : 2 * DEVS, :]
    turned = jnp.concatenate([real * cos - sine * sin, -(real * sin + sine * cos)], axis=1)
    waves = dot(turned, lon_ref[...])
    lane = lane_index(waves.shape)
    number = row_index(waves.shape) + DEVS * ((lane % (LANES // 2)) % WAVES)
    weight = jnp.where(number == 0, 1.0 / NLON, 2.0 / NLON)
    waves = jnp.where(number <= cut, waves * weight, 0.0)
    back = dot(waves, back_lon_ref[...])
    real, imag = back[:, : 2 * LANES], back[:, 2 * LANES :]
    cos, sin = twiddle_ref[2 * DEVS : 3 * DEVS, :], twiddle_ref[3 * DEVS :, :]
    turned = jnp.concatenate([real * cos - imag * sin, real * sin + imag * cos], axis=0)
    smooth = dot(back_dev_ref[...], turned)
    out_ref[:, 0, :] = smooth[:, :LANES]
    out_ref[:, 1, :] = smooth[:, LANES:]
    edge = in_ref[:, 2, :]
    right = pltpu.roll(edge, 1, 0)
    left = pltpu.roll(edge, DEVS - 1, 0)
    out_ref[:, 2, :] = jnp.where(me < FIELDS * TILES, right, left)
    out_ref[:, 3, :] = pltpu.roll(in_ref[:, 3, :], DEVS - 1, 0)


def final_kernel(c_ref, zc_ref, mc_ref, inner_ref, rest_ref, mine_ref, theirs_ref, back_ref, out_ref, adj_ref, fil_ref):
    level, inner, outer = level_signs()
    core = level % 2
    partner = jnp.where(core == 0, 1.0, 0.0).astype(jnp.float32)
    adj_ref[3, pair_half(core)] = mine_ref[...]
    adj_ref[3, pair_half(1 - core)] = theirs_ref[...]
    shape = (LON, TILES, LANES)

    def part(ref, at):
        return ref[at : at + FULL, :].reshape(shape)

    turned = jnp.concatenate(
        [back_ref[:POLAR, 0, :], back_ref[POLAR:, 1, :], back_ref[:POLAR, 1, :], back_ref[POLAR:, 0, :]], axis=0
    ).T
    lane = lane_index((LON, LANES))
    halos = []
    for f in range(FIELDS):
        value = c_ref[f] + inner * part(inner_ref, FIELDS * PACK + f * FULL) + outer * part(rest_ref, f * FULL)
        if f == 3:
            below = c_ref[2] + partner * part(inner_ref, FIELDS * (PACK + FULL)) + adj_ref[3]
            value = value - COUPLE_B * below
        adj_ref[f] = value
        fil_ref[f] = value
        ring = turned[f * HALF : (f + 1) * HALF]
        ring = jnp.concatenate([ring, pltpu.roll(ring, LANES // 2, 1)], axis=0)
        halos.append((ring[0:1], ring[LON + 1 : LON + 2]))
        ring = pltpu.roll(ring, ROWS - 1, 0)[:LON]
        fil_ref[f, :, 0, :] = jnp.where(lane < POLAR, ring, adj_ref[f, :, 0, :])
        fil_ref[f, :, TILES - 1, :] = jnp.where(lane >= LANES - POLAR, ring, adj_ref[f, :, TILES - 1, :])

    polar = polar_mask((TILES, LANES))

    def edge_fluxes(side):
        tiles = []
        for f in range(FIELDS):
            q = (side * FIELDS + f) * TILES
            tiles.append(back_ref[q : q + TILES, 2, :] if q < DEVS else back_ref[q - DEVS : q - DEVS + TILES, 3, :])
        ring = zonal_fluxes(tiles[0], [h[side] for h in halos])
        return [jnp.where(polar, a, b)[None] for a, b in zip(ring, tiles)]

    west, east = edge_fluxes(0), edge_fluxes(1)
    lane, tile = lane_index(shape), row_index(shape)
    for f in range(FIELDS):
        field = fil_ref[f]
        zonal = zc_ref[...] * field
        merid = mc_ref[...] * field
        if f == 0:
            zonal = zonal + COUPLE_H * fil_ref[3]
        if f == 1:
            merid = merid + COUPLE_H * fil_ref[3]
        if f == 3:
            zonal = zonal + COUPLE_G * fil_ref[0]
            merid = merid + COUPLE_G * fil_ref[1]
        after = jnp.concatenate([zonal[1:], east[f]], axis=0)
        before = jnp.concatenate([west[f], zonal[:-1]], axis=0)
        north = pltpu.roll(merid, LANES - 1, 2)
        carry = jnp.where(tile == TILES - 1, 0.0, pltpu.roll(north, TILES - 1, 1))
        north = jnp.where(lane == LANES - 1, carry, north)
        south = pltpu.roll(merid, 1, 2)
        carry = jnp.where(tile == 0, 0.0, pltpu.roll(south, 1, 1))
        south = jnp.where(lane == 0, carry, south)
        out_ref[f] = adj_ref[f] + (after - before) + (north - south)


def call(kernel, out_shape, *args, spaces={}, scratch=(), vmem_mib=8):
    specs = [pl.BlockSpec(memory_space=spaces.get(i, pltpu.VMEM)) for i in range(len(args))]
    return pl.pallas_call(
        kernel,
        out_shape=out_shape,
        in_specs=specs,
        out_specs=jax.tree.map(lambda _: pl.BlockSpec(memory_space=pltpu.VMEM), out_shape),
        scratch_shapes=scratch,
        compiler_params=pltpu.CompilerParams(vmem_limit_bytes=vmem_mib * 2**20),
        cost_estimate=pl.CostEstimate(flops=2**20, bytes_accessed=6 * 2**20, transcendentals=0),
    )(*args)


def array(*shape):
    return jax.ShapeDtypeStruct(shape, jnp.float32)


def body(cotangent, zonal_coef, merid_coef, vertical_wind, cutoff):
    cotangent = cotangent.reshape(FIELDS, LON, TILES, LANES)
    zonal_coef, merid_coef, vertical_wind = (
        a.reshape(LON, TILES, LANES) for a in (zonal_coef, merid_coef, vertical_wind)
    )
    inner, outer, rest, own, theta, below = call(
        pack_kernel,
        (
            array(FIELDS * (PACK + FULL) + FULL, LANES),
            array(FIELDS * PACK, LANES),
            array(FIELDS * FULL, LANES),
            array(FIELDS * PACK, LANES),
            array(LEVS, PACK, LANES),
            array(LON, TILES, LANES),
        ),
        cotangent,
        vertical_wind,
    )
    pairs = [(k, k ^ 1) for k in range(LEVS)]
    crossing = [(k, ((k + 1) ^ 1) - 1) for k in range(1, LEVS - 1)]
    inner = lax.ppermute(inner, "lev", pairs)
    outer = lax.ppermute(outer, "lev", crossing)

    def exchange(values, axis):
        return lax.cond(
            cutoff[0] > 0, lambda x: lax.all_to_all(x, axis, 0, 0, tiled=True), lambda x: jnp.zeros_like(x), values
        )

    def hand_down(values, levels):
        return lax.ppermute(values, "lev", [(k, k - levels) for k in range(levels, LEVS)])

    theta = lax.all_to_all(theta, "lev", 0, 0, tiled=True)
    pair = call(pair_kernel, array(SHARE, TILES, LANES), below, inner)
    one = hand_down(pair, 2)
    sent = call(merge_kernel, array(DEVS, 4, LANES), own, zonal_coef, inner, outer, theta)
    sent, one = lax.optimization_barrier((sent, one))
    two = hand_down(pair + one, 4)
    circle = exchange(sent, "lon")
    circle, rest, two = lax.optimization_barrier((circle, rest, two))
    rest = lax.ppermute(rest, "lev", crossing)
    smooth = call(
        filter_kernel, array(DEVS, 4, LANES), cutoff, circle, *filter_tables(), spaces={0: pltpu.SMEM}
    )
    back = lax.all_to_all(smooth, "lon", 0, 0, tiled=True)
    mine = one + two
    theirs = lax.ppermute(mine, "lev", pairs)
    out = call(
        final_kernel,
        array(FIELDS, LON, TILES, LANES),
        cotangent,
        zonal_coef,
        merid_coef,
        inner,
        rest,
        mine,
        theirs,
        back,
        scratch=[pltpu.VMEM((FIELDS, LON, TILES, LANES), jnp.float32)] * 2,
        vmem_mib=24,
    )
    return out.reshape(FIELDS, 1, LON, NLAT)


def solution(mesh):
    return jax.shard_map(
        body,
        mesh=mesh,
        in_specs=(
            P(None, "lev", "lon", None),
            P("lev", "lon", None),
            P("lev", "lon", None),
            P("lev", "lon", None),
            P(),
        ),
        out_specs=P(None, "lev", "lon", None),
        check_vma=False,
    )
```

```python
import math

import jax
import jax.numpy as jnp
import numpy as np
from jax import lax
from jax.experimental import pallas as pl
from jax.experimental.pallas import tpu as pltpu
from jax.sharding import PartitionSpec as P

NLON = 2880
LON = 45
DEVS = NLON // LON
LEVS = 8
NLAT = 1024
POLAR = 32
FIELDS = 5
LANES = 128
TILES = NLAT // LANES
SHARE = (LON + 1) // 2
HALF = 24
ROWS = 2 * HALF
PACK = HALF + 2 * TILES
FULL = TILES * LON
INSIDE = FULL - 2 * TILES
WAVES = 6

COUPLE_G = 0.3
COUPLE_H = 0.3
COUPLE_B = 0.2

HIGHEST = lax.Precision.HIGHEST


def lane_index(shape):
    return lax.broadcasted_iota(jnp.int32, shape, len(shape) - 1)


def row_index(shape):
    return lax.broadcasted_iota(jnp.int32, shape, len(shape) - 2)


def polar_mask(shape):
    lane, tile = lane_index(shape), row_index(shape) % TILES
    return ((tile == 0) & (lane < POLAR)) | ((tile == TILES - 1) & (lane >= LANES - POLAR))


def pack_polar(first, last):
    lane = lane_index((LON, LANES))
    both = jnp.where(lane < LANES // 2, first, last)
    both = jnp.concatenate([both, jnp.zeros((ROWS - LON, LANES), both.dtype)], axis=0)
    lane = lane[:HALF]
    outer = (lane < POLAR) | (lane >= LANES - POLAR)
    return jnp.where(outer, both[:HALF], pltpu.roll(both[HALF:], LANES // 2, 1))


def pack_kernel(c_ref, w_ref, inner_ref, outer_ref, rest_ref, own_ref, theta_ref, below_ref):
    rows = [slice(f * PACK, f * PACK + HALF) for f in range(FIELDS)]
    lows = [slice(f * PACK + HALF, f * PACK + HALF + TILES) for f in range(FIELDS)]
    highs = [slice(f * PACK + HALF + TILES, (f + 1) * PACK) for f in range(FIELDS)]
    w = w_ref[...]
    w_first, w_last = w_ref[:, 0, :], w_ref[:, TILES - 1, :]
    for f in range(FIELDS):
        field = c_ref[f]
        first, last = c_ref[f, :, 0, :], c_ref[f, :, TILES - 1, :]
        own_ref[rows[f], :] = pack_polar(first, last)
        own_ref[lows[f], :] = field[0]
        own_ref[highs[f], :] = field[LON - 1]
        if f == 2:
            packed = own_ref[f * PACK : (f + 1) * PACK, :]
            for k in range(LEVS):
                theta_ref[k] = packed
            inner_ref[FIELDS * (PACK + FULL) :, :] = field.reshape(FULL, LANES)
            below_ref[...] = field
        weighted = w * field
        whole = weighted.reshape(FULL, LANES)
        polar = pack_polar(w_first * first, w_last * last)
        at = FIELDS * PACK + f * FULL
        inner_ref[at : at + FULL, :] = whole
        for ref in (inner_ref, outer_ref):
            ref[rows[f], :] = polar
            ref[lows[f], :] = weighted[0]
            ref[highs[f], :] = weighted[LON - 1]
        rest_ref[f * INSIDE : (f + 1) * INSIDE, :] = whole[TILES : FULL - TILES]


def level_signs():
    level = lax.axis_index("lev")
    even = level % 2 == 0
    inner = jnp.where(even, 1.0, -1.0).astype(jnp.float32)
    outer = jnp.where((level == 0) | (level == LEVS - 1), 0.0, -inner).astype(jnp.float32)
    return level, inner, outer


def below_sum(level, value_of):
    total = jnp.where(level <= 0, value_of(0), 0.0)
    for m in range(1, LEVS):
        total = total + jnp.where(m >= level, value_of(m), 0.0)
    return total


def zonal_fluxes(coef, field):
    flux = [coef * x for x in field]
    flux[0] = flux[0] + COUPLE_H * field[3]
    flux[3] = flux[3] + COUPLE_G * field[0]
    return flux


def pair_half(core):
    return pl.ds((LON - SHARE) * core, SHARE)


def pair_kernel(below_ref, inner_ref, pair_ref):
    core = lax.axis_index("lev") % 2
    other = inner_ref[FIELDS * (PACK + FULL) :, :].reshape(LON, TILES, LANES)
    both = below_ref[...] + other
    pair_ref[...] = jnp.where(core == 0, both[:SHARE], both[LON - SHARE :])


def merge_kernel(own_ref, zc_ref, inner_ref, outer_ref, theta_ref, out_ref):
    level, inner, outer = level_signs()
    adjoint = []
    for f in range(FIELDS):
        at = slice(f * PACK, (f + 1) * PACK)
        adjoint.append(own_ref[at, :] + inner * inner_ref[at, :] + outer * outer_ref[at, :])
    adjoint[3] = adjoint[3] - COUPLE_B * below_sum(level, lambda m: theta_ref[m])
    rows = [a[:HALF] for a in adjoint]
    rows.append(jnp.zeros((LANES - FIELDS * HALF, LANES), jnp.float32))
    turned = jnp.concatenate(rows, axis=0).T
    out_ref[:POLAR, 0, :] = turned[:POLAR]
    out_ref[POLAR:, 0, :] = turned[LANES - POLAR :]
    out_ref[:POLAR, 1, :] = turned[2 * POLAR : 3 * POLAR]
    out_ref[POLAR:, 1, :] = turned[POLAR : 2 * POLAR]
    coef = jnp.concatenate([zc_ref[0], zc_ref[LON - 1]], axis=0)
    flux = zonal_fluxes(coef, [a[HALF:] for a in adjoint])
    flux[0] = jnp.where(polar_mask(coef.shape), coef, flux[0])
    edges = jnp.concatenate([x[TILES:] for x in flux] + [x[:TILES] for x in flux], axis=0)
    out_ref[:, 2, :] = edges[:DEVS]
    left = 2 * FIELDS * TILES - DEVS
    out_ref[:left, 3, :] = edges[DEVS:]
    out_ref[left:, 3, :] = jnp.zeros((DEVS - left, LANES), jnp.float32)


def filter_tables():
    dev = np.arange(DEVS)
    lane = np.arange(2 * LANES)
    place = (lane % LANES) % HALF + HALF * (lane // LANES)
    used = (lane % LANES) < FIELDS * HALF
    field = np.where(used, (lane % LANES) // HALF, -1)
    wave_field = np.arange(LANES // 2) // WAVES
    wave = np.arange(LANES // 2) % WAVES
    circle = 2 * math.pi * np.outer(dev, dev) / DEVS

    def twiddle(offset):
        angle = 2 * math.pi * np.outer(dev, place + offset) / NLON
        return np.concatenate([np.cos(angle), np.sin(angle)], axis=0)

    def short(offset, keep):
        angle = 2 * math.pi * np.outer(place + offset, wave) / LON
        same = (field[:, None] == wave_field[None, :]) & keep[:, None]
        return np.cos(angle) * same, np.sin(angle) * same

    inside = used & (place < LON)
    cos_in, sin_in = short(0, inside)
    cos_out, sin_out = short(-1, used)
    forward_dev = np.concatenate([np.cos(circle), np.sin(circle)], axis=0)
    forward_lon = np.concatenate(
        [np.concatenate([cos_in, -sin_in], 1), np.concatenate([sin_in, cos_in], 1)], axis=0
    )
    back_lon = np.concatenate(
        [np.concatenate([cos_out.T, sin_out.T], 1), np.concatenate([-sin_out.T, cos_out.T], 1)], axis=0
    )
    back_dev = np.concatenate([np.cos(circle), -np.sin(circle)], axis=1)
    tables = (forward_dev, np.concatenate([twiddle(0), twiddle(-1)], 0), forward_lon, back_lon, back_dev)
    return [np.asarray(t, np.float32) for t in tables]


def dot(a, b):
    return jnp.dot(a, b, precision=HIGHEST, preferred_element_type=jnp.float32)


def filter_kernel(cut_ref, in_ref, dev_ref, twiddle_ref, lon_ref, back_lon_ref, back_dev_ref, out_ref):
    me = lax.axis_index("lon")
    cut = cut_ref[me]
    values = jnp.concatenate([in_ref[:, 0, :], in_ref[:, 1, :]], axis=1)
    split = dot(dev_ref[...], values)
    real, sine = split[:DEVS], split[DEVS:]
    cos, sin = twiddle_ref[:DEVS, :], twiddle_ref[DEVS : 2 * DEVS, :]
    turned = jnp.concatenate([real * cos - sine * sin, -(real * sin + sine * cos)], axis=1)
    waves = dot(turned, lon_ref[...])
    lane = lane_index(waves.shape)
    number = row_index(waves.shape) + DEVS * ((lane % (LANES // 2)) % WAVES)
    weight = jnp.where(number == 0, 1.0 / NLON, 2.0 / NLON)
    waves = jnp.where(number <= cut, waves * weight, 0.0)
    back = dot(waves, back_lon_ref[...])
    real, imag = back[:, : 2 * LANES], back[:, 2 * LANES :]
    cos, sin = twiddle_ref[2 * DEVS : 3 * DEVS, :], twiddle_ref[3 * DEVS :, :]
    turned = jnp.concatenate([real * cos - imag * sin, real * sin + imag * cos], axis=0)
    smooth = dot(back_dev_ref[...], turned)
    out_ref[:, 0, :] = smooth[:, :LANES]
    out_ref[:, 1, :] = smooth[:, LANES:]
    edge = in_ref[:, 2, :]
    right = pltpu.roll(edge, 1, 0)
    left = pltpu.roll(edge, DEVS - 1, 0)
    out_ref[:, 2, :] = jnp.where(me < FIELDS * TILES, right, left)
    out_ref[:, 3, :] = pltpu.roll(in_ref[:, 3, :], DEVS - 1, 0)


def final_kernel(c_ref, zc_ref, mc_ref, inner_ref, outer_ref, rest_ref, mine_ref, theirs_ref, back_ref, out_ref, adj_ref, fil_ref):
    level, inner, outer = level_signs()
    core = level % 2
    partner = jnp.where(core == 0, 1.0, 0.0).astype(jnp.float32)
    adj_ref[3, pair_half(core)] = mine_ref[...]
    adj_ref[3, pair_half(1 - core)] = theirs_ref[...]
    shape = (LON, TILES, LANES)

    def part(ref, at):
        return ref[at : at + FULL, :].reshape(shape)

    turned = jnp.concatenate(
        [back_ref[:POLAR, 0, :], back_ref[POLAR:, 1, :], back_ref[:POLAR, 1, :], back_ref[POLAR:, 0, :]], axis=0
    ).T
    lane = lane_index((LON, LANES))
    halos = []
    for f in range(FIELDS):
        at = f * PACK + HALF
        pieces = [outer_ref[at : at + TILES, :], rest_ref[f * INSIDE : (f + 1) * INSIDE, :]]
        pieces.append(outer_ref[at + TILES : at + 2 * TILES, :])
        other = jnp.concatenate(pieces, axis=0).reshape(shape)
        value = c_ref[f] + inner * part(inner_ref, FIELDS * PACK + f * FULL) + outer * other
        if f == 3:
            below = c_ref[2] + partner * part(inner_ref, FIELDS * (PACK + FULL)) + adj_ref[3]
            value = value - COUPLE_B * below
        adj_ref[f] = value
        fil_ref[f] = value
        ring = turned[f * HALF : (f + 1) * HALF]
        ring = jnp.concatenate([ring, pltpu.roll(ring, LANES // 2, 1)], axis=0)
        halos.append((ring[0:1], ring[LON + 1 : LON + 2]))
        ring = pltpu.roll(ring, ROWS - 1, 0)[:LON]
        fil_ref[f, :, 0, :] = jnp.where(lane < POLAR, ring, adj_ref[f, :, 0, :])
        fil_ref[f, :, TILES - 1, :] = jnp.where(lane >= LANES - POLAR, ring, adj_ref[f, :, TILES - 1, :])

    polar = polar_mask((TILES, LANES))

    def edge_fluxes(side):
        tiles = []
        for f in range(FIELDS):
            q = (side * FIELDS + f) * TILES
            tiles.append(back_ref[q : q + TILES, 2, :] if q < DEVS else back_ref[q - DEVS : q - DEVS + TILES, 3, :])
        ring = zonal_fluxes(tiles[0], [h[side] for h in halos])
        return [jnp.where(polar, a, b)[None] for a, b in zip(ring, tiles)]

    west, east = edge_fluxes(0), edge_fluxes(1)
    lane, tile = lane_index(shape), row_index(shape)
    for f in range(FIELDS):
        field = fil_ref[f]
        zonal = zc_ref[...] * field
        merid = mc_ref[...] * field
        if f == 0:
            zonal = zonal + COUPLE_H * fil_ref[3]
        if f == 1:
            merid = merid + COUPLE_H * fil_ref[3]
        if f == 3:
            zonal = zonal + COUPLE_G * fil_ref[0]
            merid = merid + COUPLE_G * fil_ref[1]
        after = jnp.concatenate([zonal[1:], east[f]], axis=0)
        before = jnp.concatenate([west[f], zonal[:-1]], axis=0)
        north = pltpu.roll(merid, LANES - 1, 2)
        carry = jnp.where(tile == TILES - 1, 0.0, pltpu.roll(north, TILES - 1, 1))
        north = jnp.where(lane == LANES - 1, carry, north)
        south = pltpu.roll(merid, 1, 2)
        carry = jnp.where(tile == 0, 0.0, pltpu.roll(south, 1, 1))
        south = jnp.where(lane == 0, carry, south)
        out_ref[f] = adj_ref[f] + (after - before) + (north - south)


def call(kernel, out_shape, *args, spaces={}, scratch=(), vmem_mib=8):
    specs = [pl.BlockSpec(memory_space=spaces.get(i, pltpu.VMEM)) for i in range(len(args))]
    return pl.pallas_call(
        kernel,
        out_shape=out_shape,
        in_specs=specs,
        out_specs=jax.tree.map(lambda _: pl.BlockSpec(memory_space=pltpu.VMEM), out_shape),
        scratch_shapes=scratch,
        compiler_params=pltpu.CompilerParams(vmem_limit_bytes=vmem_mib * 2**20),
        cost_estimate=pl.CostEstimate(flops=2**20, bytes_accessed=6 * 2**20, transcendentals=0),
    )(*args)


def array(*shape):
    return jax.ShapeDtypeStruct(shape, jnp.float32)


def body(cotangent, zonal_coef, merid_coef, vertical_wind, cutoff):
    cotangent = cotangent.reshape(FIELDS, LON, TILES, LANES)
    zonal_coef, merid_coef, vertical_wind = (
        a.reshape(LON, TILES, LANES) for a in (zonal_coef, merid_coef, vertical_wind)
    )
    inner, outer, rest, own, theta, below = call(
        pack_kernel,
        (
            array(FIELDS * (PACK + FULL) + FULL, LANES),
            array(FIELDS * PACK, LANES),
            array(FIELDS * INSIDE, LANES),
            array(FIELDS * PACK, LANES),
            array(LEVS, PACK, LANES),
            array(LON, TILES, LANES),
        ),
        cotangent,
        vertical_wind,
    )
    pairs = [(k, k ^ 1) for k in range(LEVS)]
    crossing = [(k, ((k + 1) ^ 1) - 1) for k in range(1, LEVS - 1)]
    inner = lax.ppermute(inner, "lev", pairs)
    outer = lax.ppermute(outer, "lev", crossing)

    def exchange(values, axis):
        return lax.cond(
            cutoff[0] > 0, lambda x: lax.all_to_all(x, axis, 0, 0, tiled=True), lambda x: jnp.zeros_like(x), values
        )

    def hand_down(values, levels):
        return lax.ppermute(values, "lev", [(k, k - levels) for k in range(levels, LEVS)])

    theta = lax.all_to_all(theta, "lev", 0, 0, tiled=True)
    pair = call(pair_kernel, array(SHARE, TILES, LANES), below, inner)
    one = hand_down(pair, 2)
    sent = call(merge_kernel, array(DEVS, 4, LANES), own, zonal_coef, inner, outer, theta)
    sent, one = lax.optimization_barrier((sent, one))
    two = hand_down(pair + one, 4)
    circle = exchange(sent, "lon")
    circle, rest, two = lax.optimization_barrier((circle, rest, two))
    rest = lax.ppermute(rest, "lev", crossing)
    smooth = call(
        filter_kernel, array(DEVS, 4, LANES), cutoff, circle, *filter_tables(), spaces={0: pltpu.SMEM}
    )
    back = lax.all_to_all(smooth, "lon", 0, 0, tiled=True)
    mine = one + two
    theirs = lax.ppermute(mine, "lev", pairs)
    out = call(
        final_kernel,
        array(FIELDS, LON, TILES, LANES),
        cotangent,
        zonal_coef,
        merid_coef,
        inner,
        outer,
        rest,
        mine,
        theirs,
        back,
        scratch=[pltpu.VMEM((FIELDS, LON, TILES, LANES), jnp.float32)] * 2,
        vmem_mib=24,
    )
    return out.reshape(FIELDS, 1, LON, NLAT)


def solution(mesh):
    return jax.shard_map(
        body,
        mesh=mesh,
        in_specs=(
            P(None, "lev", "lon", None),
            P("lev", "lon", None),
            P("lev", "lon", None),
            P("lev", "lon", None),
            P(),
        ),
        out_specs=P(None, "lev", "lon", None),
        check_vma=False,
    )
```
